256 devices in a mesh: row: 64 (over z, y, core), tm: 4 (over x).
Axes of the slice: x: 4, y: 4, z: 8, core: 2. Of those that a mesh axis runs over, the one named last changes fastest.
Arguments:
- snapshots: float32 [524288, 512], P('row', 'tm'), may hold values from -16 to 16
- modes: float32 [524288, 32], P('row'), may hold values from -6 to 6
- ridge: float32 [528], replicated, may hold values from 0.0005 to 0.005
Outputs:
- correction: float32 [524288, 528], P(('row', 'tm'))
The draws below stay inside these ranges and needn't reach their ends.
All inputs are finite; a program needn't handle non-finite values.
Results may differ from the reference program's by a relative error of at most 0.0003.
Values sent between devices are 32-bit elements; how exact they have to be, the bound alone decides.
A program may use at most 128 MiB of HBM per device.

```python
import math
import jax
import jax.numpy as jnp
import numpy as np
from jax import lax

R = 32
FEAT = 528
NODES = 524288
TIMES = 512


def basis_field(key):
    return jnp.clip(jax.random.normal(jax.random.fold_in(key, 11), (NODES, R), jnp.float32), -6.0, 6.0)


def draw_modes(key, part):
    return basis_field(key)


def draw_snapshots(key, part):
    basis = basis_field(key)
    coefs = 0.2 * jax.random.normal(jax.random.fold_in(key, 13), (R, TIMES), jnp.float32)
    noise = 0.5 * jax.random.normal(jax.random.fold_in(key, 14), (NODES, TIMES), jnp.float32)
    field = jnp.dot(basis, coefs, precision=lax.Precision.HIGHEST) + noise
    return jnp.clip(field, -16.0, 16.0)


def setup_inputs(seed: int = 0) -> dict:
    keys = jax.random.split(jax.random.key(seed), 4)
    return {
        "snapshots": draw_snapshots(jax.random.fold_in(keys[3], 71), 0),
        "modes": draw_modes(jax.random.fold_in(keys[3], 71), 0),
        "ridge": jnp.clip(jnp.exp(jax.random.uniform(keys[2], (FEAT,), jnp.float32, math.log(0.0005), math.log(0.005))), 0.0005, 0.005),
    }


def reference(snapshots, modes, ridge):
    high = lax.Precision.HIGHEST
    first, second = np.triu_indices(R)
    coords = jnp.dot(modes.T.astype(jnp.float32), snapshots.astype(jnp.float32), precision=high, preferred_element_type=jnp.float32) / NODES
    feats = coords[first] * coords[second]
    resid = snapshots - jnp.dot(modes.astype(jnp.float32), coords.astype(jnp.float32), precision=high, preferred_element_type=jnp.float32)
    gram = jnp.dot(feats.astype(jnp.float32), feats.T.astype(jnp.float32), precision=high, preferred_element_type=jnp.float32) + TIMES * jnp.diag(ridge)
    factor = jnp.linalg.cholesky(gram)
    identity = jnp.eye(FEAT, dtype=gram.dtype)
    factor_inv = jax.scipy.linalg.solve_triangular(factor, identity, lower=True)
    inverse = jnp.dot(factor_inv.T.astype(jnp.float32), factor_inv.astype(jnp.float32), precision=high, preferred_element_type=jnp.float32)
    cross = lax.dot_general(resid.astype(jnp.float32), feats.astype(jnp.float32), (((1,), (1,)), ((), ())), precision=high, preferred_element_type=jnp.float32)
    return jnp.dot(cross.astype(jnp.float32), inverse.astype(jnp.float32), precision=high, preferred_element_type=jnp.float32)
```

```python
import functools

import jax
import jax.numpy as jnp
import numpy as np
from jax import lax
from jax.experimental import pallas as pl
from jax.experimental.pallas import tpu as pltpu
from jax.sharding import PartitionSpec as P

R = 32
FEAT = R * (R + 1) // 2
F32 = jnp.float32
BF16 = jnp.bfloat16
LOW_LIMIT = 128.0
LOW_STOP = 0.05
FINE_STOP = 1e-3
FINE_MAX = 12


def split2(x):
    hi = x.astype(BF16)
    return hi, (x - hi.astype(F32)).astype(BF16)


def split3(x):
    hi = x.astype(BF16)
    rest = x - hi.astype(F32)
    mid = rest.astype(BF16)
    return hi, mid, (rest - mid.astype(F32)).astype(BF16)


def dot(a, b, dims=((1,), (0,))):
    return lax.dot_general(a, b, (dims, ((), ())), preferred_element_type=F32)


def dot3(a, b, dims=((1,), (0,))):
    ah, al = a
    bh, bl = b
    return dot(al, bh, dims) + dot(ah, bl, dims) + dot(ah, bh, dims)


def dot6(a, b, dims=((1,), (0,))):
    ah, am, al = a
    bh, bm, bl = b
    small = dot(al, bh, dims) + dot(ah, bl, dims) + dot(am, bm, dims)
    return small + (dot(am, bh, dims) + dot(ah, bm, dims)) + dot(ah, bh, dims)


def weights_kernel(coords_ref, scale_ref, wh_ref, wl_ref, packed_ref, feats, hmat, xmat):
    times = hmat.shape[0]
    coords = jnp.concatenate([coords_ref[c] for c in range(coords_ref.shape[0])], axis=1)
    ch, cm, cl = split3(coords)
    packed_ref[...] = jnp.concatenate([ch, cm, cl, ch, cm, ch], axis=0)
    start = 0
    for i in range(R):
        feats[start : start + R - i, :] = (
            coords[i : i + 1, :] * coords[i:, :] * scale_ref[start : start + R - i, :]
        )
        start += R - i
    scaled = feats[...]
    eye = (
        lax.broadcasted_iota(jnp.int32, (times, times), 0)
        == lax.broadcasted_iota(jnp.int32, (times, times), 1)
    ).astype(F32)
    hmat[...] = eye + dot6(split3(scaled.T), split3(scaled))
    upper = jnp.max(jnp.sum(jnp.abs(hmat[...]), axis=0, keepdims=True))
    first = 2.0 / (1.0 + upper)
    rho = (upper - 1.0) * first * 0.5
    gain = 2.0 / (2.0 - rho * rho)
    xmat[...] = (gain * first) * (2.0 * eye - first * hmat[...])
    rho = rho * rho * 0.5 * gain

    def low_step(rho):
        gain = 2.0 / (2.0 - rho * rho)
        x = xmat[...].astype(BF16)
        turn = 2.0 * eye - dot(hmat[...].astype(BF16), x)
        xmat[...] = gain * dot(x, turn.astype(BF16))
        return rho * rho * 0.5 * gain

    def high_step(rho):
        gain = 2.0 / (2.0 - rho * rho)
        x = split3(xmat[...])
        turn = 2.0 * eye - dot6(split3(hmat[...]), x)
        xmat[...] = gain * dot6(x, split3(turn))
        return rho * rho * 0.5 * gain

    easy = upper <= LOW_LIMIT
    rho = lax.while_loop(lambda r: jnp.logical_and(easy, r > LOW_STOP), low_step, rho)
    rho = lax.while_loop(lambda r: r > LOW_STOP, high_step, rho)

    def fine_step(state):
        step, _ = state
        x = xmat[...]
        rest = eye - dot6(split3(hmat[...]), split3(x))
        size = jnp.max(jnp.sum(jnp.abs(rest), axis=0, keepdims=True))
        xmat[...] = x + dot3(split2(x), split2(rest))
        return step + 1, size

    lax.while_loop(
        lambda s: jnp.logical_and(s[0] < FINE_MAX, s[1] > FINE_STOP),
        fine_step,
        (jnp.int32(0), jnp.float32(1.0)),
    )
    w = dot6(split3(feats[...]), split3(xmat[...])) * scale_ref[...]
    wh, wl = split2(w)
    wh_ref[...] = wh
    wl_ref[...] = wl


def weights(coords, ridge):
    times = coords.shape[0] * coords.shape[2]
    root = lax.rsqrt(ridge * times)
    vmem = pl.BlockSpec(memory_space=pltpu.VMEM)
    return pl.pallas_call(
        weights_kernel,
        out_shape=[jax.ShapeDtypeStruct((FEAT, times), BF16)] * 2
        + [jax.ShapeDtypeStruct((6 * R, times), BF16)],
        in_specs=[vmem] * 2,
        out_specs=[vmem] * 3,
        scratch_shapes=[
            pltpu.VMEM((FEAT, times), F32),
            pltpu.VMEM((times, times), F32),
            pltpu.VMEM((times, times), F32),
        ],
        compiler_params=pltpu.CompilerParams(vmem_limit_bytes=48 * 2**20),
        cost_estimate=pl.CostEstimate(
            flops=2 * times**3 * 60, bytes_accessed=4 * times * FEAT, transcendentals=0
        ),
    )(coords, root[:, None])


def correction_kernel(blocks_ref, modes_ref, coords_ref, wh_ref, wl_ref, out_ref):
    snaps = jnp.concatenate([blocks_ref[b] for b in range(blocks_ref.shape[0])], axis=1)
    resid = snaps - dot(modes_ref[...], coords_ref[...])
    rh, rl = split2(resid)
    last = ((1,), (1,))
    wh = wh_ref[...]
    out_ref[...] = dot(wh, rl, last) + dot(wl_ref[...], rh, last) + dot(wh, rh, last)


def exact_split3(x):
    hi = lax.reduce_precision(x, 8, 7)
    mid = lax.reduce_precision(x - hi, 8, 7)
    low = x - hi - mid
    return hi.astype(BF16), mid.astype(BF16), low.astype(BF16)


def correct(blocks, modes6, coords6, wh, wl, tile=512):
    parts, count, width = blocks.shape
    times = parts * width
    depth = modes6.shape[1]
    return pl.pallas_call(
        correction_kernel,
        grid=(count // tile,),
        out_shape=jax.ShapeDtypeStruct((FEAT, count), F32),
        in_specs=[
            pl.BlockSpec((parts, tile, width), lambda i: (0, i, 0)),
            pl.BlockSpec((tile, depth), lambda i: (i, 0)),
            pl.BlockSpec((depth, times), lambda i: (0, 0)),
            pl.BlockSpec((FEAT, times), lambda i: (0, 0)),
            pl.BlockSpec((FEAT, times), lambda i: (0, 0)),
        ],
        out_specs=pl.BlockSpec((FEAT, tile), lambda i: (0, i)),
        compiler_params=pltpu.CompilerParams(vmem_limit_bytes=32 * 2**20),
        cost_estimate=pl.CostEstimate(
            flops=2 * count * times * FEAT * 3, bytes_accessed=12 * 2**20, transcendentals=0
        ),
    )(blocks, modes6, coords6, wh, wl)


GROUP = 8
MESH = pl.DeviceIdType.MESH


def project_kernel(modes_ref, snaps_ref, out_ref):
    @pl.when(pl.program_id(0) == 0)
    def _():
        out_ref[...] = jnp.zeros_like(out_ref)

    both = jnp.concatenate(split2(modes_ref[...]), axis=0)
    sh, sl = split2(snaps_ref[...])
    found = dot(both, sl) + dot(both, sh)
    out_ref[...] += found[R:] + found[:R]


def project(modes_t, snaps, step=2048):
    nodes, width = snaps.shape
    return pl.pallas_call(
        project_kernel,
        grid=(nodes // step,),
        out_shape=jax.ShapeDtypeStruct((R, width), F32),
        in_specs=[
            pl.BlockSpec((R, step), lambda i: (0, i)),
            pl.BlockSpec((step, width), lambda i: (i, 0)),
        ],
        out_specs=pl.BlockSpec((R, width), lambda i: (0, 0)),
        compiler_params=pltpu.CompilerParams(vmem_limit_bytes=32 * 2**20),
        cost_estimate=pl.CostEstimate(
            flops=6 * nodes * R * width, bytes_accessed=5 * 2**20, transcendentals=0
        ),
    )(modes_t, snaps)


def coords_kernel(scale, *refs):
    cols = len(refs) - 11
    parts, out_ref = refs[:cols], refs[cols]
    part, near, far, whole = refs[cols + 1 : cols + 5]
    near_send, near_recv, far_send, far_recv, whole_send, whole_recv = refs[cols + 5 :]
    row, col = lax.axis_index("row"), lax.axis_index("tm")
    planes = far.shape[0]
    plane, spot = row // GROUP, row % GROUP

    def near_peer(k):
        return {"row": plane * GROUP + (spot + k) % GROUP}

    def far_peer(k):
        return {"row": ((plane + k) % planes) * GROUP + spot}

    barrier = pltpu.get_barrier_semaphore()

    def greet(peer):
        pl.semaphore_signal(barrier, inc=1, device_id=peer, device_id_type=MESH)

    lax.fori_loop(1, GROUP, lambda k, _: greet(near_peer(k)), None)
    lax.fori_loop(1, planes, lambda k, _: greet(far_peer(k)), None)
    for c in range(cols):
        for s in range(GROUP):
            part[s, c] = parts[c][4 * s : 4 * s + 4, :]
    pl.semaphore_wait(barrier, GROUP - 1 + planes - 1)

    def near_copy(k):
        return pltpu.make_async_remote_copy(
            src_ref=part.at[(spot + k) % GROUP], dst_ref=near.at[spot],
            send_sem=near_send.at[k], recv_sem=near_recv.at[k],
            device_id=near_peer(k), device_id_type=MESH,
        )

    def far_copy(k):
        return pltpu.make_async_remote_copy(
            src_ref=far.at[plane], dst_ref=far.at[plane],
            send_sem=far_send.at[k], recv_sem=far_recv.at[k],
            device_id=far_peer(k), device_id_type=MESH,
        )

    def whole_copy(k):
        return pltpu.make_async_remote_copy(
            src_ref=whole.at[spot], dst_ref=whole.at[spot],
            send_sem=whole_send.at[k], recv_sem=whole_recv.at[k],
            device_id=near_peer(k), device_id_type=MESH,
        )

    lax.fori_loop(1, GROUP, lambda k, _: near_copy(k).start(), None)
    near[spot] = part[spot]
    lax.fori_loop(1, GROUP, lambda k, _: near_copy(k).wait_recv(), None)
    far[plane] = jnp.sum(near[...], axis=0)
    lax.fori_loop(1, planes, lambda k, _: far_copy(k).start(), None)
    lax.fori_loop(1, GROUP, lambda k, _: near_copy(k).wait_send(), None)
    lax.fori_loop(1, planes, lambda k, _: far_copy(k).wait_recv(), None)
    whole[spot] = jnp.sum(far[...], axis=0) * scale
    lax.fori_loop(1, GROUP, lambda k, _: whole_copy(k).start(), None)
    lax.fori_loop(1, planes, lambda k, _: far_copy(k).wait_send(), None)
    lax.fori_loop(1, GROUP, lambda k, _: whole_copy(k).wait(), None)
    for c in range(cols):
        place = (col + cols - c) % cols
        for s in range(GROUP):
            out_ref[place, 4 * s : 4 * s + 4, :] = whole[s, c]


def all_coords(parts, nodes_total):
    cols = len(parts)
    planes = lax.axis_size("row") // GROUP
    rows, width = parts[0].shape
    piece = (cols, rows // GROUP, width)
    dma = pltpu.SemaphoreType.DMA
    vmem = pl.BlockSpec(memory_space=pltpu.VMEM)
    return pl.pallas_call(
        functools.partial(coords_kernel, 1.0 / nodes_total),
        out_shape=jax.ShapeDtypeStruct((cols, rows, width), F32),
        in_specs=[vmem] * cols,
        out_specs=vmem,
        scratch_shapes=[
            pltpu.VMEM((GROUP,) + piece, F32),
            pltpu.VMEM((GROUP,) + piece, F32),
            pltpu.VMEM((planes,) + piece, F32),
            pltpu.VMEM((GROUP,) + piece, F32),
            dma((GROUP,)), dma((GROUP,)),
            dma((planes,)), dma((planes,)),
            dma((GROUP,)), dma((GROUP,)),
        ],
        compiler_params=pltpu.CompilerParams(collective_id=0, has_side_effects=True),
        cost_estimate=pl.CostEstimate(flops=10**6, bytes_accessed=2**20, transcendentals=0),
    )(*parts)


def shards(snapshots, modes, ridge):
    nodes_total = modes.shape[0] * lax.axis_size("row")
    parts = lax.axis_size("tm")
    count = snapshots.shape[0] // parts
    pieces = snapshots.reshape(parts, count, -1)
    mine = project(modes.T, snapshots)
    gathered = [mine] + [
        lax.ppermute(mine, "tm", [(i, (i + k) % parts) for i in range(parts)])
        for k in range(1, parts)
    ]
    gathered, pieces = lax.optimization_barrier((gathered, pieces))
    blocks = lax.all_to_all(pieces, "tm", split_axis=0, concat_axis=0, tiled=False)
    coords = all_coords(gathered, nodes_total)
    wh, wl, coords6 = weights(coords, ridge)
    sub = lax.dynamic_slice_in_dim(modes, lax.axis_index("tm") * count, count, 0)
    sub, _ = lax.optimization_barrier((sub, mine))
    mh, mm, ml = exact_split3(sub)
    modes6 = jnp.concatenate([mh, mh, mh, mm, mm, ml], axis=1)
    return correct(blocks, modes6, coords6, wh, wl).T


def solution(mesh):
    return jax.shard_map(
        shards,
        mesh=mesh,
        in_specs=(P("row", "tm"), P("row", None), P()),
        out_specs=P(("row", "tm"), None),
        check_vma=False,
    )
```

```python
import functools

import jax
import jax.numpy as jnp
import numpy as np
from jax import lax
from jax.experimental import pallas as pl
from jax.experimental.pallas import tpu as pltpu
from jax.sharding import PartitionSpec as P

R = 32
FEAT = R * (R + 1) // 2
F32 = jnp.float32
BF16 = jnp.bfloat16
COARSE_STEPS = 5
FINE_STEPS = 2
FINE_STOP = 4e-3
HIGH_STOP = 0.05
FINE_MAX = 12
GROUP = 8
TILE = 512
CHUNKS = ((0, 256), (256, 256), (512, 512), (1024, 512), (1536, 512))
EARLY_CHUNKS = 1
MESH = pl.DeviceIdType.MESH


def split2(x):
    hi = x.astype(BF16)
    return hi, (x - hi.astype(F32)).astype(BF16)


def split3(x):
    hi = x.astype(BF16)
    rest = x - hi.astype(F32)
    mid = rest.astype(BF16)
    return hi, mid, (rest - mid.astype(F32)).astype(BF16)


def dot(a, b, dims=((1,), (0,))):
    return lax.dot_general(a, b, (dims, ((), ())), preferred_element_type=F32)


def dot3(a, b, dims=((1,), (0,))):
    ah, al = a
    bh, bl = b
    return dot(al, bh, dims) + dot(ah, bl, dims) + dot(ah, bh, dims)


def dot6(a, b, dims=((1,), (0,))):
    ah, am, al = a
    bh, bm, bl = b
    small = dot(al, bh, dims) + dot(ah, bl, dims) + dot(am, bm, dims)
    return small + (dot(am, bh, dims) + dot(ah, bm, dims)) + dot(ah, bh, dims)


def identity(size):
    down = lax.broadcasted_iota(jnp.int32, (size, size), 0)
    return (down == lax.broadcasted_iota(jnp.int32, (size, size), 1)).astype(F32)


def column_scale(ridge_ref, times):
    row = lax.rsqrt(ridge_ref[...] * times)
    return jnp.sum(identity(FEAT) * row, axis=1, keepdims=True)


def pack6(parts):
    hi, mid, low = parts
    return jnp.concatenate([hi, mid, low, hi, mid, hi], axis=0)


def fill_feats(coords, scale, feats):
    start = 0
    for i in range(R):
        feats[start : start + R - i, :] = (
            coords[i : i + 1, :] * coords[i:, :] * scale[start : start + R - i, :]
        )
        start += R - i


def first_guess(feats, hmat, xmat):
    eye = identity(hmat.shape[0])
    scaled = feats[...]
    hmat[...] = eye + dot6(split3(scaled.T), split3(scaled))
    upper = jnp.max(jnp.sum(jnp.abs(hmat[...]), axis=0, keepdims=True), axis=1, keepdims=True)
    first = 2.0 / (1.0 + upper)
    rho = (upper - 1.0) * first * 0.5
    gain = 2.0 / (2.0 - rho * rho)
    xmat[...] = (gain * first) * (2.0 * eye - first * hmat[...])
    return rho * rho * 0.5 * gain


def coarse_step(hmat, xmat, rho):
    gain = 2.0 / (2.0 - rho * rho)
    x = xmat[...].astype(BF16)
    turn = 2.0 * identity(hmat.shape[0]) - dot(hmat[...].astype(BF16), x)
    xmat[...] = gain * dot(x, turn.astype(BF16))
    return rho * rho * 0.5 * gain


def high_step(hmat, xmat, rho):
    gain = 2.0 / (2.0 - rho * rho)
    x = split3(xmat[...])
    turn = 2.0 * identity(hmat.shape[0]) - dot6(split3(hmat[...]), x)
    xmat[...] = gain * dot6(x, split3(turn))
    return rho * rho * 0.5 * gain


def fine_step(hmat, xmat):
    x = xmat[...]
    rest = identity(hmat.shape[0]) - dot6(split3(hmat[...]), split3(x))
    xmat[...] = x + dot3(split2(x), split2(rest))
    return jnp.max(jnp.sum(jnp.abs(rest), axis=0, keepdims=True), axis=1, keepdims=True)


def store_weights(feats, xmat, scale, wh_ref, wl_ref):
    wh, wl = split2(dot6(split3(feats[...]), split3(xmat[...])) * scale)
    wh_ref[...] = wh
    wl_ref[...] = wl


def corrected(snaps, modes_t, packed, wh, wl):
    mh, mm, ml = split3(modes_t)
    modes6 = jnp.concatenate([mh, mh, mh, mm, mm, ml], axis=0)
    resid = snaps - dot(modes6, packed, ((0,), (0,)))
    rh, rl = split2(resid)
    last = ((1,), (1,))
    return dot(wh, rl, last) + dot(wl, rh, last) + dot(wh, rh, last)


def main_kernel(nodes_total, done_tiles, snaps_ref, modes_ref, ridge_ref, *refs):
    outs = 5 + (done_tiles > 0)
    blocks_ref, coords_ref, wh_ref, wl_ref, size_ref = refs[:5]
    out_ref = refs[5] if done_tiles else None
    (
        snaps, modes_t, cross, near, far, whole, feats, hmat, xmat, packed, tiles, result,
        load_sem, cross_send, cross_recv, near_send, near_recv, far_send, far_recv,
        whole_send, whole_recv, block_send, block_recv, tile_sem, result_sem,
    ) = refs[outs:]
    row, col = lax.axis_index("row"), lax.axis_index("tm")
    cols, planes = cross.shape[0], far.shape[0]
    plane, spot = row // GROUP, row % GROUP
    count = snaps.shape[0] // cols
    times = hmat.shape[0]

    def cross_peer(k):
        return {"tm": (col + k) % cols}

    def near_peer(k):
        return {"row": plane * GROUP + (spot + k) % GROUP}

    def far_peer(k):
        return {"row": ((plane + k) % planes) * GROUP + spot}

    def remote(src, dst, send, recv, peer):
        return pltpu.make_async_remote_copy(
            src_ref=src, dst_ref=dst, send_sem=send, recv_sem=recv,
            device_id=peer, device_id_type=MESH,
        )

    def block_copy(k, c):
        start, size = CHUNKS[c]
        source = snaps_ref.at[pl.ds(((col + k) % cols) * count + start, size), :]
        return remote(
            source, blocks_ref.at[k - 1, pl.ds(start, size), :],
            block_send.at[k, c], block_recv.at[k, c], cross_peer(k),
        )

    def cross_copy(k):
        return remote(cross.at[0], cross.at[k], cross_send.at[k], cross_recv.at[k], cross_peer(k))

    def near_copy(k):
        return remote(
            cross.at[:, (spot + k) % GROUP], near.at[spot],
            near_send.at[k], near_recv.at[k], near_peer(k),
        )

    def far_copy(k):
        return remote(far.at[plane], far.at[plane], far_send.at[k], far_recv.at[k], far_peer(k))

    def whole_copy(k):
        return remote(
            whole.at[spot], whole.at[spot], whole_send.at[k], whole_recv.at[k], near_peer(k)
        )

    def load(c):
        rows = pl.ds(c * count, count)
        return pltpu.make_async_copy(snaps_ref.at[rows, :], snaps.at[rows, :], load_sem.at[c])

    modes_load = pltpu.make_async_copy(modes_ref, modes_t, load_sem.at[cols])
    modes_load.start()
    for c in range(cols):
        load(c).start()
    barrier = pltpu.get_barrier_semaphore()
    peers = [cross_peer(k) for k in range(1, cols)]
    peers += [near_peer(k) for k in range(1, GROUP)] + [far_peer(k) for k in range(1, planes)]
    for peer in peers:
        pl.semaphore_signal(barrier, inc=1, device_id=peer, device_id_type=MESH)
    pl.semaphore_wait(barrier, len(peers))

    order = [1, cols - 1] + list(range(2, cols - 1))
    for c in range(EARLY_CHUNKS):
        for k in order:
            block_copy(k, c).start()

    modes_load.wait()
    total = jnp.zeros((2 * R, snaps.shape[1]), F32)
    for c in range(cols):
        load(c).wait()
        both = jnp.concatenate(split2(modes_t[:, c * count : (c + 1) * count]), axis=0)
        sh, sl = split2(snaps[c * count : (c + 1) * count, :])
        total += dot(both, sl) + dot(both, sh)
    mine = total[R:] + total[:R]
    share = R // GROUP
    for s in range(GROUP):
        cross[0, s] = mine[share * s : share * (s + 1), :]
    for k in order:
        cross_copy(k).start()
    for c in range(EARLY_CHUNKS, len(CHUNKS)):
        for k in order:
            block_copy(k, c).start()
    scale = column_scale(ridge_ref, times)
    for k in order:
        cross_copy(k).wait_recv()
    for k in range(1, GROUP):
        near_copy(k).start()
    near[spot] = cross[:, spot]
    for k in range(1, GROUP):
        near_copy(k).wait_recv()
    far[plane] = jnp.sum(near[...], axis=0)
    for k in range(1, planes):
        far_copy(k).start()
    for k in range(1, planes):
        far_copy(k).wait_recv()
    whole[spot] = jnp.sum(far[...], axis=0) * (1.0 / nodes_total)
    for k in range(1, GROUP):
        whole_copy(k).start()
    for k in range(1, GROUP):
        whole_copy(k).wait_recv()
    width = snaps.shape[1]
    for c in range(cols):
        for s in range(GROUP):
            coords_ref[share * s : share * (s + 1), c * width : (c + 1) * width] = whole[s, c]

    coords = coords_ref[...]
    packed[...] = pack6(split3(coords))
    fill_feats(coords, scale, feats)
    rho = first_guess(feats, hmat, xmat)
    rho = lax.fori_loop(0, COARSE_STEPS, lambda _, r: coarse_step(hmat, xmat, r), rho)
    size = lax.fori_loop(0, FINE_STEPS, lambda _, r: fine_step(hmat, xmat), rho)
    size_ref[...] = jnp.broadcast_to(size, size_ref.shape)
    store_weights(feats, xmat, scale, wh_ref, wl_ref)

    for t in range(len(CHUNKS)):
        start, size = CHUNKS[t]
        for k in order:
            block_copy(k, t).wait_recv()
        if start + size > done_tiles * TILE or (start + size) % TILE:
            continue
        tile = (start + size) // TILE - 1
        rows = pl.ds(tile * TILE, TILE)
        moves = [
            pltpu.make_async_copy(
                blocks_ref.at[k - 1, rows, :], tiles.at[k - 1], tile_sem.at[k]
            )
            for k in range(1, cols)
        ]
        for move in moves:
            move.start()
        for move in moves:
            move.wait()
        base = pl.multiple_of(col * count + tile * TILE, TILE)
        values = jnp.concatenate(
            [snaps[pl.ds(base, TILE), :]] + [tiles[k] for k in range(cols - 1)], axis=1
        )
        result[tile] = corrected(
            values, modes_t[:, pl.ds(base, TILE)], packed[...], wh_ref[...], wl_ref[...]
        )
        pltpu.make_async_copy(
            result.at[tile], out_ref.at[:, pl.ds(tile * TILE, TILE)], result_sem.at[tile]
        ).start()
    for tile in range(done_tiles):
        pltpu.make_async_copy(
            result.at[tile], out_ref.at[:, pl.ds(tile * TILE, TILE)], result_sem.at[tile]
        ).wait()
    for k in range(1, cols):
        cross_copy(k).wait_send()
        for c in range(len(CHUNKS)):
            block_copy(k, c).wait_send()
    for k in range(1, GROUP):
        near_copy(k).wait_send()
        whole_copy(k).wait_send()
    for k in range(1, planes):
        far_copy(k).wait_send()


def exchange_and_weigh(snapshots, modes_t, ridge, nodes_total, done_tiles):
    cols = lax.axis_size("tm")
    planes = lax.axis_size("row") // GROUP
    nodes, width = snapshots.shape
    count, times = nodes // cols, cols * width
    piece = (cols, R // GROUP, width)
    dma = pltpu.SemaphoreType.DMA
    vmem = pl.BlockSpec(memory_space=pltpu.VMEM)
    far_away = pl.BlockSpec(memory_space=pl.ANY)
    shape = jax.ShapeDtypeStruct
    out_shape = [
        shape((cols - 1, count, width), F32),
        shape((R, times), F32),
        shape((FEAT, times), BF16),
        shape((FEAT, times), BF16),
        shape((8, 128), F32),
    ]
    out_specs = [far_away, vmem, vmem, vmem, vmem]
    if done_tiles:
        out_shape.append(shape((FEAT, done_tiles * TILE), F32))
        out_specs.append(far_away)
    return pl.pallas_call(
        functools.partial(main_kernel, nodes_total, done_tiles),
        out_shape=out_shape,
        in_specs=[far_away, far_away, vmem],
        out_specs=out_specs,
        scratch_shapes=[
            pltpu.VMEM((nodes, width), F32),
            pltpu.VMEM((R, nodes), F32),
            pltpu.VMEM((cols, GROUP, R // GROUP, width), F32),
            pltpu.VMEM((GROUP,) + piece, F32),
            pltpu.VMEM((planes,) + piece, F32),
            pltpu.VMEM((GROUP,) + piece, F32),
            pltpu.VMEM((FEAT, times), F32),
            pltpu.VMEM((times, times), F32),
            pltpu.VMEM((times, times), F32),
            pltpu.VMEM((6 * R, times), BF16),
            pltpu.VMEM((cols - 1, TILE, width), F32),
            pltpu.VMEM((max(done_tiles, 1), FEAT, TILE), F32),
            dma((cols + 1,)),
            dma((cols,)), dma((cols,)),
            dma((GROUP,)), dma((GROUP,)),
            dma((planes,)), dma((planes,)),
            dma((GROUP,)), dma((GROUP,)),
            dma((cols, len(CHUNKS))), dma((cols, len(CHUNKS))),
            dma((cols,)),
            dma((max(done_tiles, 1),)),
        ],
        compiler_params=pltpu.CompilerParams(
            collective_id=0, has_side_effects=True, vmem_limit_bytes=44 * 2**20
        ),
        cost_estimate=pl.CostEstimate(flops=10**10, bytes_accessed=2**24, transcendentals=0),
    )(snapshots, modes_t, ridge.reshape(1, -1))


def final_kernel(done_tiles, place_ref, *refs):
    if done_tiles:
        done_ref, refs = refs[0], refs[1:]
    own_ref, blocks_ref, modes_ref, coords_ref, wh_ref, wl_ref, size_ref, ridge_ref = refs[:8]
    out_ref, wh_slow, wl_slow, feats, hmat, xmat, flag = refs[8:]
    step = pl.program_id(0)
    times = hmat.shape[0]

    @pl.when(step == 0)
    def _():
        good = jnp.max(size_ref[...]) <= FINE_STOP
        flag[0] = good.astype(jnp.int32)

        @pl.when(jnp.logical_not(good))
        def _():
            scale = column_scale(ridge_ref, times)
            fill_feats(coords_ref[...], scale, feats)
            rho = jnp.max(first_guess(feats, hmat, xmat))
            lax.while_loop(
                lambda r: r > HIGH_STOP, lambda r: high_step(hmat, xmat, r), rho
            )

            lax.while_loop(
                lambda s: jnp.logical_and(s[0] < FINE_MAX, s[1] > FINE_STOP),
                lambda s: (s[0] + 1, jnp.max(fine_step(hmat, xmat))),
                (jnp.int32(0), jnp.float32(1.0)),
            )
            store_weights(feats, xmat, scale, wh_slow, wl_slow)

    def compute(wh, wl):
        parts = [own_ref[...]] + [blocks_ref[k] for k in range(blocks_ref.shape[0])]
        out_ref[...] = corrected(
            jnp.concatenate(parts, axis=1), modes_ref[...], pack6(split3(coords_ref[...])),
            wh[...], wl[...],
        )

    good = flag[0] == 1

    @pl.when(jnp.logical_not(good))
    def _():
        compute(wh_slow, wl_slow)

    @pl.when(jnp.logical_and(good, step >= done_tiles))
    def _():
        compute(wh_ref, wl_ref)

    if done_tiles:

        @pl.when(jnp.logical_and(good, step < done_tiles))
        def _():
            out_ref[...] = done_ref[...]


def finish(done_tiles, place, done, snapshots, modes_t, ridge, blocks, coords, wh, wl, size):
    parts, count, width = blocks.shape
    times = (parts + 1) * width
    tiles = count // TILE
    fixed = lambda i, place: (0, 0)
    in_specs, args = [], ()
    if done_tiles:
        in_specs = [
            pl.BlockSpec((FEAT, TILE), lambda i, place: (0, jnp.minimum(i, done_tiles - 1)))
        ]
        args = (done,)
    in_specs += [
        pl.BlockSpec((TILE, width), lambda i, place: (place[0] * tiles + i, 0)),
        pl.BlockSpec((parts, TILE, width), lambda i, place: (0, i, 0)),
        pl.BlockSpec((R, TILE), lambda i, place: (0, place[0] * tiles + i)),
        pl.BlockSpec((R, times), fixed),
        pl.BlockSpec((FEAT, times), fixed),
        pl.BlockSpec((FEAT, times), fixed),
        pl.BlockSpec((8, 128), fixed),
        pl.BlockSpec((1, FEAT), fixed),
    ]
    args += (snapshots, blocks, modes_t, coords, wh, wl, size, ridge.reshape(1, -1))
    return pl.pallas_call(
        functools.partial(final_kernel, done_tiles),
        grid_spec=pltpu.PrefetchScalarGridSpec(
            num_scalar_prefetch=1,
            grid=(tiles,),
            in_specs=in_specs,
            out_specs=pl.BlockSpec((FEAT, TILE), lambda i, place: (0, i)),
            scratch_shapes=[
                pltpu.VMEM((FEAT, times), BF16),
                pltpu.VMEM((FEAT, times), BF16),
                pltpu.VMEM((FEAT, times), F32),
                pltpu.VMEM((times, times), F32),
                pltpu.VMEM((times, times), F32),
                pltpu.SMEM((1,), jnp.int32),
            ],
        ),
        out_shape=jax.ShapeDtypeStruct((FEAT, count), F32),
        compiler_params=pltpu.CompilerParams(vmem_limit_bytes=32 * 2**20),
        cost_estimate=pl.CostEstimate(
            flops=2 * count * times * FEAT * 3, bytes_accessed=12 * 2**20, transcendentals=0
        ),
    )(place, *args)


DONE_TILES = 3


def shards(snapshots, modes, ridge):
    nodes_total = modes.shape[0] * lax.axis_size("row")
    modes_t = modes.T
    found = exchange_and_weigh(snapshots, modes_t, ridge, nodes_total, DONE_TILES)
    blocks, coords, wh, wl, size = found[:5]
    done = found[5] if DONE_TILES else None
    place = lax.axis_index("tm").astype(jnp.int32).reshape(1)
    return finish(
        DONE_TILES, place, done, snapshots, modes_t, ridge, blocks, coords, wh, wl, size
    ).T


def solution(mesh):
    return jax.shard_map(
        shards,
        mesh=mesh,
        in_specs=(P("row", "tm"), P("row", None), P()),
        out_specs=P(("row", "tm"), None),
        check_vma=False,
    )
```

```python
import functools

import jax
import jax.numpy as jnp
import numpy as np
from jax import lax
from jax.experimental import pallas as pl
from jax.experimental.pallas import tpu as pltpu
from jax.sharding import PartitionSpec as P

R = 32
FEAT = R * (R + 1) // 2
F32 = jnp.float32
BF16 = jnp.bfloat16
COARSE_STEPS = 5
FINE_STEPS = 2
FINE_STOP = 4e-3
HIGH_STOP = 0.05
FINE_MAX = 12
GROUP = 8
TILE = 256
CHUNKS = ((0, 256), (256, 256), (512, 512), (1024, 512), (1536, 256), (1792, 256))
EARLY_CHUNKS = 1
DONE = (0, 1792)
MESH = pl.DeviceIdType.MESH


def split2(x):
    hi = x.astype(BF16)
    return hi, (x - hi.astype(F32)).astype(BF16)


def split3(x):
    hi = x.astype(BF16)
    rest = x - hi.astype(F32)
    mid = rest.astype(BF16)
    return hi, mid, (rest - mid.astype(F32)).astype(BF16)


def dot(a, b, dims=((1,), (0,))):
    return lax.dot_general(a, b, (dims, ((), ())), preferred_element_type=F32)


def dot3(a, b, dims=((1,), (0,))):
    ah, al = a
    bh, bl = b
    return dot(al, bh, dims) + dot(ah, bl, dims) + dot(ah, bh, dims)


def dot6(a, b, dims=((1,), (0,))):
    ah, am, al = a
    bh, bm, bl = b
    small = dot(al, bh, dims) + dot(ah, bl, dims) + dot(am, bm, dims)
    return small + (dot(am, bh, dims) + dot(ah, bm, dims)) + dot(ah, bh, dims)


def identity(size):
    down = lax.broadcasted_iota(jnp.int32, (size, size), 0)
    return (down == lax.broadcasted_iota(jnp.int32, (size, size), 1)).astype(F32)


def column_scale(ridge_ref, times):
    row = lax.rsqrt(ridge_ref[...].reshape(1, FEAT) * times)
    return jnp.sum(identity(FEAT) * row, axis=1, keepdims=True)


def pack6(parts):
    hi, mid, low = parts
    return jnp.concatenate([hi, mid, low, hi, mid, hi], axis=0)


def fill_feats(coords, scale, feats):
    start = 0
    for i in range(R):
        feats[start : start + R - i, :] = (
            coords[i : i + 1, :] * coords[i:, :] * scale[start : start + R - i, :]
        )
        start += R - i


def first_guess(feats, hmat, xmat):
    eye = identity(hmat.shape[0])
    scaled = feats[...]
    hmat[...] = eye + dot6(split3(scaled.T), split3(scaled))
    upper = jnp.max(jnp.sum(jnp.abs(hmat[...]), axis=0, keepdims=True), axis=1, keepdims=True)
    first = 2.0 / (1.0 + upper)
    rho = (upper - 1.0) * first * 0.5
    gain = 2.0 / (2.0 - rho * rho)
    xmat[...] = (gain * first) * (2.0 * eye - first * hmat[...])
    return rho * rho * 0.5 * gain


def coarse_step(hmat, xmat, rho):
    gain = 2.0 / (2.0 - rho * rho)
    x = xmat[...].astype(BF16)
    turn = 2.0 * identity(hmat.shape[0]) - dot(hmat[...].astype(BF16), x)
    xmat[...] = gain * dot(x, turn.astype(BF16))
    return rho * rho * 0.5 * gain


def high_step(hmat, xmat, rho):
    gain = 2.0 / (2.0 - rho * rho)
    x = split3(xmat[...])
    turn = 2.0 * identity(hmat.shape[0]) - dot6(split3(hmat[...]), x)
    xmat[...] = gain * dot6(x, split3(turn))
    return rho * rho * 0.5 * gain


def fine_step(hmat, xmat):
    x = xmat[...]
    rest = identity(hmat.shape[0]) - dot6(split3(hmat[...]), split3(x))
    xmat[...] = x + dot3(split2(x), split2(rest))
    return jnp.max(jnp.sum(jnp.abs(rest), axis=0, keepdims=True), axis=1, keepdims=True)


def store_weights(feats, xmat, scale, wh_ref, wl_ref):
    wh, wl = split2(dot6(split3(feats[...]), split3(xmat[...])) * scale)
    wh_ref[...] = wh
    wl_ref[...] = wl


def corrected(snaps, modes_t, packed, wh, wl):
    mh, mm, ml = split3(modes_t)
    modes6 = jnp.concatenate([mh, mh, mh, mm, mm, ml], axis=0)
    resid = snaps - dot(modes6, packed, ((0,), (0,)))
    rh, rl = split2(resid)
    last = ((1,), (1,))
    return dot(wh, rl, last) + dot(wl, rh, last) + dot(wh, rh, last)


def main_kernel(nodes_total, snaps_ref, modes_ref, ridge_hbm, *refs):
    (
        blocks_ref, coords_ref, wh_ref, wl_ref, size_ref, done_ref,
        snaps, modes_t, cross, near, far, whole, feats, hmat, xmat, packed,
        load_sem, cross_send, cross_recv, near_send, near_recv, far_send, far_recv,
        whole_send, whole_recv, block_send, block_recv, ridge_ref, ridge_sem,
    ) = refs
    row, col = lax.axis_index("row"), lax.axis_index("tm")
    cols, planes = cross.shape[0], far.shape[0]
    plane, spot = row // GROUP, row % GROUP
    count = snaps.shape[0] // cols
    times = hmat.shape[0]

    def cross_peer(k):
        return {"tm": (col + k) % cols}

    def near_peer(k):
        return {"row": plane * GROUP + (spot + k) % GROUP}

    def far_peer(k):
        return {"row": ((plane + k) % planes) * GROUP + spot}

    def remote(src, dst, send, recv, peer):
        return pltpu.make_async_remote_copy(
            src_ref=src, dst_ref=dst, send_sem=send, recv_sem=recv,
            device_id=peer, device_id_type=MESH,
        )

    def block_copy(k, c):
        start, size = CHUNKS[c]
        source = snaps_ref.at[pl.ds(((col + k) % cols) * count + start, size), :]
        return remote(
            source, blocks_ref.at[k - 1, pl.ds(start, size), :],
            block_send.at[k, c], block_recv.at[k, c], cross_peer(k),
        )

    def cross_copy(k):
        return remote(cross.at[0], cross.at[k], cross_send.at[k], cross_recv.at[k], cross_peer(k))

    def near_copy(k):
        return remote(
            cross.at[:, (spot + k) % GROUP], near.at[spot],
            near_send.at[k], near_recv.at[k], near_peer(k),
        )

    def far_copy(k):
        return remote(far.at[plane], far.at[plane], far_send.at[k], far_recv.at[k], far_peer(k))

    def whole_copy(k):
        return remote(
            whole.at[spot], whole.at[spot], whole_send.at[k], whole_recv.at[k], near_peer(k)
        )

    def load(c):
        rows = pl.ds(c * count, count)
        return pltpu.make_async_copy(snaps_ref.at[rows, :], snaps.at[rows, :], load_sem.at[c])

    modes_load = pltpu.make_async_copy(modes_ref, modes_t, load_sem.at[cols])
    modes_load.start()
    ridge_load = pltpu.make_async_copy(ridge_hbm, ridge_ref, ridge_sem)
    ridge_load.start()
    for c in range(cols):
        load(c).start()
    barrier = pltpu.get_barrier_semaphore()
    peers = [cross_peer(k) for k in range(1, cols)]
    peers += [near_peer(k) for k in range(1, GROUP)] + [far_peer(k) for k in range(1, planes)]
    for peer in peers:
        pl.semaphore_signal(barrier, inc=1, device_id=peer, device_id_type=MESH)
    pl.semaphore_wait(barrier, len(peers))

    order = [1, cols - 1] + list(range(2, cols - 1))
    for c in range(EARLY_CHUNKS):
        for k in order:
            block_copy(k, c).start()

    modes_load.wait()
    total = jnp.zeros((2 * R, snaps.shape[1]), F32)
    for c in range(cols):
        load(c).wait()
        both = jnp.concatenate(split2(modes_t[:, c * count : (c + 1) * count]), axis=0)
        sh, sl = split2(snaps[c * count : (c + 1) * count, :])
        total += dot(both, sl) + dot(both, sh)
    mine = total[R:] + total[:R]
    share = R // GROUP
    for s in range(GROUP):
        cross[0, s] = mine[share * s : share * (s + 1), :]
    for k in order:
        cross_copy(k).start()
    for c in range(EARLY_CHUNKS, len(CHUNKS)):
        for k in order:
            block_copy(k, c).start()
    ridge_load.wait()
    scale = column_scale(ridge_ref, times)
    for k in order:
        cross_copy(k).wait_recv()
    for k in range(1, GROUP):
        near_copy(k).start()
    near[spot] = cross[:, spot]
    for k in range(1, GROUP):
        near_copy(k).wait_recv()
    far[plane] = jnp.sum(near[...], axis=0)
    for k in range(1, planes):
        far_copy(k).start()
    for k in range(1, planes):
        far_copy(k).wait_recv()
    whole[spot] = jnp.sum(far[...], axis=0) * (1.0 / nodes_total)
    for k in range(1, GROUP):
        whole_copy(k).start()
    for k in range(1, GROUP):
        whole_copy(k).wait_recv()
    width = snaps.shape[1]
    for c in range(cols):
        for s in range(GROUP):
            coords_ref[share * s : share * (s + 1), c * width : (c + 1) * width] = whole[s, c]

    coords = coords_ref[...]
    packed[...] = pack6(split3(coords))
    fill_feats(coords, scale, feats)
    rho = first_guess(feats, hmat, xmat)
    rho = lax.fori_loop(0, COARSE_STEPS, lambda _, r: coarse_step(hmat, xmat, r), rho)
    size = lax.fori_loop(0, FINE_STEPS, lambda _, r: fine_step(hmat, xmat), rho)
    size_ref[...] = jnp.broadcast_to(size, size_ref.shape)
    store_weights(feats, xmat, scale, wh_ref, wl_ref)

    for t in range(len(CHUNKS)):
        start, size = CHUNKS[t]
        for k in order:
            block_copy(k, t).wait_recv()
        if start < DONE[0] or start >= DONE[1]:
            continue
        base = pl.multiple_of(col * count + start, TILE)
        values = [snaps[pl.ds(base, size), :]]
        values += [blocks_ref[k, start : start + size, :] for k in range(cols - 1)]
        done_ref[:, start - DONE[0] : start - DONE[0] + size] = corrected(
            jnp.concatenate(values, axis=1), modes_t[:, pl.ds(base, size)], packed[...],
            wh_ref[...], wl_ref[...],
        )
    for k in range(1, cols):
        cross_copy(k).wait_send()
        for c in range(len(CHUNKS)):
            block_copy(k, c).wait_send()
    for k in range(1, GROUP):
        near_copy(k).wait_send()
        whole_copy(k).wait_send()
    for k in range(1, planes):
        far_copy(k).wait_send()


def exchange_and_weigh(snapshots, modes_t, ridge, nodes_total):
    cols = lax.axis_size("tm")
    planes = lax.axis_size("row") // GROUP
    nodes, width = snapshots.shape
    count, times = nodes // cols, cols * width
    piece = (cols, R // GROUP, width)
    dma = pltpu.SemaphoreType.DMA
    vmem = pl.BlockSpec(memory_space=pltpu.VMEM)
    far_away = pl.BlockSpec(memory_space=pltpu.HBM)
    shape = jax.ShapeDtypeStruct
    return pl.pallas_call(
        functools.partial(main_kernel, nodes_total),
        out_shape=[
            shape((cols - 1, count, width), F32),
            shape((R, times), F32),
            shape((FEAT, times), BF16),
            shape((FEAT, times), BF16),
            shape((8, 128), F32),
            shape((FEAT, DONE[1] - DONE[0]), F32),
        ],
        in_specs=[far_away] * 3,
        out_specs=[vmem] * 6,
        scratch_shapes=[
            pltpu.VMEM((nodes, width), F32),
            pltpu.VMEM((R, nodes), F32),
            pltpu.VMEM((cols, GROUP, R // GROUP, width), F32),
            pltpu.VMEM((GROUP,) + piece, F32),
            pltpu.VMEM((planes,) + piece, F32),
            pltpu.VMEM((GROUP,) + piece, F32),
            pltpu.VMEM((FEAT, times), F32),
            pltpu.VMEM((times, times), F32),
            pltpu.VMEM((times, times), F32),
            pltpu.VMEM((6 * R, times), BF16),
            dma((cols + 1,)),
            dma((cols,)), dma((cols,)),
            dma((GROUP,)), dma((GROUP,)),
            dma((planes,)), dma((planes,)),
            dma((GROUP,)), dma((GROUP,)),
            dma((cols, len(CHUNKS))), dma((cols, len(CHUNKS))),
            pltpu.VMEM((FEAT,), F32), dma,
        ],
        compiler_params=pltpu.CompilerParams(
            collective_id=0, has_side_effects=True, vmem_limit_bytes=44 * 2**20
        ),
        cost_estimate=pl.CostEstimate(flops=10**10, bytes_accessed=2**24, transcendentals=0),
    )(snapshots, modes_t, ridge)


def final_kernel(
    snaps_ref, modes_ref, ridge_ref, blocks_ref, coords_ref, wh_ref, wl_ref, size_ref, done_ref,
    *refs,
):
    early, refs = refs[:-12], refs[-12:]
    (
        out_ref, own, modes_t, result, wh_slow, wl_slow, feats, hmat, xmat,
        load_sem, done_sem, result_sem,
    ) = refs
    times = hmat.shape[0]
    parts, count, _ = blocks_ref.shape
    tiles = count // TILE
    first = lax.axis_index("tm") * count
    rest = [t for t in range(tiles) if not DONE[0] <= t * TILE < DONE[1]]

    def moves(slot, tile):
        rows = pl.ds(pl.multiple_of(first + tile * TILE, TILE), TILE)
        return (
            pltpu.make_async_copy(snaps_ref.at[rows, :], own.at[slot], load_sem.at[slot, 0]),
            pltpu.make_async_copy(modes_ref.at[:, rows], modes_t.at[slot], load_sem.at[slot, 1]),
        )

    def store(slot, tile):
        columns = pl.ds(pl.multiple_of(tile * TILE, TILE), TILE)
        return pltpu.make_async_copy(
            result.at[slot], out_ref.at[:, columns], result_sem.at[slot]
        )

    def compute(slot, tile, wh, wl):
        rows = pl.ds(pl.multiple_of(tile * TILE, TILE), TILE)
        if early and isinstance(tile, int) and tile == 0:
            others = [block[...] for block in early]
        else:
            others = [blocks_ref[k, rows, :] for k in range(parts)]
        result[slot] = corrected(
            jnp.concatenate([own[slot]] + others, axis=1), modes_t[slot],
            pack6(split3(coords_ref[...])), wh[...], wl[...],
        )

    good = jnp.max(size_ref[...]) <= FINE_STOP

    @pl.when(good)
    def _():
        copy = pltpu.make_async_copy(
            done_ref, out_ref.at[:, pl.ds(DONE[0], DONE[1] - DONE[0])], done_sem
        )
        for slot, tile in enumerate(rest):
            for move in moves(slot, tile):
                move.start()
        copy.start()
        for slot, tile in enumerate(rest):
            for move in moves(slot, tile):
                move.wait()
            compute(slot, tile, wh_ref, wl_ref)
            store(slot, tile).start()
        for slot, tile in enumerate(rest):
            store(slot, tile).wait()
        copy.wait()

    @pl.when(jnp.logical_not(good))
    def _():
        scale = column_scale(ridge_ref, times)
        fill_feats(coords_ref[...], scale, feats)
        rho = jnp.max(first_guess(feats, hmat, xmat))
        lax.while_loop(lambda r: r > HIGH_STOP, lambda r: high_step(hmat, xmat, r), rho)
        lax.while_loop(
            lambda s: jnp.logical_and(s[0] < FINE_MAX, s[1] > FINE_STOP),
            lambda s: (s[0] + 1, jnp.max(fine_step(hmat, xmat))),
            (jnp.int32(0), jnp.float32(1.0)),
        )
        store_weights(feats, xmat, scale, wh_slow, wl_slow)

        def whole_tile(tile):
            for move in moves(0, tile):
                move.start()
            for move in moves(0, tile):
                move.wait()
            compute(0, tile, wh_slow, wl_slow)
            store(0, tile).start()
            store(0, tile).wait()

        whole_tile(0)
        lax.fori_loop(1, tiles, lambda tile, _: whole_tile(tile), None)


def finish(snapshots, modes_t, ridge, blocks, coords, wh, wl, size, done, early):
    parts, count, width = blocks.shape
    times = (parts + 1) * width
    slots = (count - DONE[1] + DONE[0]) // TILE
    dma = pltpu.SemaphoreType.DMA
    vmem = pl.BlockSpec(memory_space=pltpu.VMEM)
    far_away = pl.BlockSpec(memory_space=pltpu.HBM)
    return pl.pallas_call(
        final_kernel,
        out_shape=jax.ShapeDtypeStruct((FEAT, count), F32),
        in_specs=[far_away, far_away] + [vmem] * (7 + len(early)),
        out_specs=far_away,
        scratch_shapes=[
            pltpu.VMEM((slots, TILE, width), F32),
            pltpu.VMEM((slots, R, TILE), F32),
            pltpu.VMEM((slots, FEAT, TILE), F32),
            pltpu.VMEM((FEAT, times), BF16),
            pltpu.VMEM((FEAT, times), BF16),
            pltpu.VMEM((FEAT, times), F32),
            pltpu.VMEM((times, times), F32),
            pltpu.VMEM((times, times), F32),
            dma((slots, 2)), dma, dma((slots,)),
        ],
        compiler_params=pltpu.CompilerParams(vmem_limit_bytes=36 * 2**20),
        cost_estimate=pl.CostEstimate(flops=10**9, bytes_accessed=2**23, transcendentals=0),
    )(snapshots, modes_t, ridge, blocks, coords, wh, wl, size, done, *early)


def shards(snapshots, modes, ridge):
    nodes_total = modes.shape[0] * lax.axis_size("row")
    modes_t = modes.T
    early = []
    found = exchange_and_weigh(snapshots, modes_t, ridge, nodes_total)
    return finish(snapshots, modes_t, ridge, *found, early).T


def solution(mesh):
    return jax.shard_map(
        shards,
        mesh=mesh,
        in_specs=(P("row", "tm"), P("row", None), P()),
        out_specs=P(("row", "tm"), None),
        check_vma=False,
    )
```

```python
import functools

import jax
import jax.numpy as jnp
import numpy as np
from jax import lax
from jax.experimental import pallas as pl
from jax.experimental.pallas import tpu as pltpu
from jax.sharding import PartitionSpec as P

R = 32
FEAT = R * (R + 1) // 2
F32 = jnp.float32
BF16 = jnp.bfloat16
COARSE_STEPS = 5
FINE_STEPS = 2
FINE_STOP = 4e-3
HIGH_STOP = 0.05
FINE_MAX = 12
GROUP = 8
TILE = 128
CHUNKS = ((0, 256), (256, 256), (512, 512), (1024, 512), (1536, 256), (1792, 128), (1920, 128))
EARLY_CHUNKS = 1
DONE = (0, 1920)
MESH = pl.DeviceIdType.MESH


def split2(x):
    hi = x.astype(BF16)
    return hi, (x - hi.astype(F32)).astype(BF16)


def split3(x):
    hi = x.astype(BF16)
    rest = x - hi.astype(F32)
    mid = rest.astype(BF16)
    return hi, mid, (rest - mid.astype(F32)).astype(BF16)


def dot(a, b, dims=((1,), (0,))):
    return lax.dot_general(a, b, (dims, ((), ())), preferred_element_type=F32)


def dot3(a, b, dims=((1,), (0,))):
    ah, al = a
    bh, bl = b
    return dot(al, bh, dims) + dot(ah, bl, dims) + dot(ah, bh, dims)


def dot6(a, b, dims=((1,), (0,))):
    ah, am, al = a
    bh, bm, bl = b
    small = dot(al, bh, dims) + dot(ah, bl, dims) + dot(am, bm, dims)
    return small + (dot(am, bh, dims) + dot(ah, bm, dims)) + dot(ah, bh, dims)


def identity(size):
    down = lax.broadcasted_iota(jnp.int32, (size, size), 0)
    return (down == lax.broadcasted_iota(jnp.int32, (size, size), 1)).astype(F32)


def column_scale(ridge_ref, times):
    row = lax.rsqrt(ridge_ref[...].reshape(1, FEAT) * times)
    return jnp.sum(identity(FEAT) * row, axis=1, keepdims=True)


def pack6(parts):
    hi, mid, low = parts
    return jnp.concatenate([hi, mid, low, hi, mid, hi], axis=0)


def fill_feats(coords, scale, feats):
    start = 0
    for i in range(R):
        feats[start : start + R - i, :] = (
            coords[i : i + 1, :] * coords[i:, :] * scale[start : start + R - i, :]
        )
        start += R - i


def first_guess(feats, hmat, xmat):
    eye = identity(hmat.shape[0])
    scaled = feats[...]
    hmat[...] = eye + dot6(split3(scaled.T), split3(scaled))
    upper = jnp.max(jnp.sum(jnp.abs(hmat[...]), axis=0, keepdims=True), axis=1, keepdims=True)
    first = 2.0 / (1.0 + upper)
    rho = (upper - 1.0) * first * 0.5
    gain = 2.0 / (2.0 - rho * rho)
    xmat[...] = (gain * first) * (2.0 * eye - first * hmat[...])
    return rho * rho * 0.5 * gain


def coarse_step(hmat, xmat, rho):
    gain = 2.0 / (2.0 - rho * rho)
    x = xmat[...].astype(BF16)
    turn = 2.0 * identity(hmat.shape[0]) - dot(hmat[...].astype(BF16), x)
    xmat[...] = gain * dot(x, turn.astype(BF16))
    return rho * rho * 0.5 * gain


def high_step(hmat, xmat, rho):
    gain = 2.0 / (2.0 - rho * rho)
    x = split3(xmat[...])
    turn = 2.0 * identity(hmat.shape[0]) - dot6(split3(hmat[...]), x)
    xmat[...] = gain * dot6(x, split3(turn))
    return rho * rho * 0.5 * gain


def fine_step(hmat, xmat):
    x = xmat[...]
    rest = identity(hmat.shape[0]) - dot6(split3(hmat[...]), split3(x))
    xmat[...] = x + dot3(split2(x), split2(rest))
    return jnp.max(jnp.sum(jnp.abs(rest), axis=0, keepdims=True), axis=1, keepdims=True)


def store_weights(feats, xmat, scale, wh_ref, wl_ref):
    wh, wl = split2(dot6(split3(feats[...]), split3(xmat[...])) * scale)
    wh_ref[...] = wh
    wl_ref[...] = wl


def corrected(snaps, modes_t, packed, wh, wl):
    mh, mm, ml = split3(modes_t)
    modes6 = jnp.concatenate([mh, mh, mh, mm, mm, ml], axis=0)
    resid = snaps - dot(modes6, packed, ((0,), (0,)))
    rh, rl = split2(resid)
    last = ((1,), (1,))
    return dot(wh, rl, last) + dot(wl, rh, last) + dot(wh, rh, last)


def main_kernel(nodes_total, snaps_ref, modes_ref, ridge_hbm, *refs):
    (
        blocks_ref, coords_ref, wh_ref, wl_ref, size_ref, done_ref,
        snaps, modes_t, cross, near, far, whole, feats, hmat, xmat, packed,
        load_sem, cross_send, cross_recv, near_send, near_recv, far_send, far_recv,
        whole_send, whole_recv, block_send, block_recv, ridge_ref, ridge_sem,
    ) = refs
    row, col = lax.axis_index("row"), lax.axis_index("tm")
    cols, planes = cross.shape[0], far.shape[0]
    plane, spot = row // GROUP, row % GROUP
    count = snaps.shape[0] // cols
    times = hmat.shape[0]

    def cross_peer(k):
        return {"tm": (col + k) % cols}

    def near_peer(k):
        return {"row": plane * GROUP + (spot + k) % GROUP}

    def far_peer(k):
        return {"row": ((plane + k) % planes) * GROUP + spot}

    def remote(src, dst, send, recv, peer):
        return pltpu.make_async_remote_copy(
            src_ref=src, dst_ref=dst, send_sem=send, recv_sem=recv,
            device_id=peer, device_id_type=MESH,
        )

    def block_copy(k, c):
        start, size = CHUNKS[c]
        source = snaps_ref.at[pl.ds(((col + k) % cols) * count + start, size), :]
        return remote(
            source, blocks_ref.at[k - 1, pl.ds(start, size), :],
            block_send.at[k, c], block_recv.at[k, c], cross_peer(k),
        )

    def cross_copy(k):
        return remote(cross.at[0], cross.at[k], cross_send.at[k], cross_recv.at[k], cross_peer(k))

    def near_copy(k):
        return remote(
            cross.at[:, (spot + k) % GROUP], near.at[spot],
            near_send.at[k], near_recv.at[k], near_peer(k),
        )

    def far_copy(k):
        return remote(far.at[plane], far.at[plane], far_send.at[k], far_recv.at[k], far_peer(k))

    def whole_copy(k):
        return remote(
            whole.at[spot], whole.at[spot], whole_send.at[k], whole_recv.at[k], near_peer(k)
        )

    def load(c):
        rows = pl.ds(c * count, count)
        return pltpu.make_async_copy(snaps_ref.at[rows, :], snaps.at[rows, :], load_sem.at[c])

    barrier = pltpu.get_barrier_semaphore()
    peers = [far_peer(k) for k in range(1, planes)] + [cross_peer(k) for k in range(1, cols)]
    peers += [near_peer(k) for k in range(1, GROUP)]
    for peer in peers:
        pl.semaphore_signal(barrier, inc=1, device_id=peer, device_id_type=MESH)
    modes_load = pltpu.make_async_copy(modes_ref, modes_t, load_sem.at[cols])
    modes_load.start()
    ridge_load = pltpu.make_async_copy(ridge_hbm, ridge_ref, ridge_sem)
    ridge_load.start()
    for c in range(cols):
        load(c).start()
    pl.semaphore_wait(barrier, len(peers))

    order = [1, cols - 1] + list(range(2, cols - 1))
    for c in range(EARLY_CHUNKS):
        for k in order:
            block_copy(k, c).start()

    modes_load.wait()
    total = jnp.zeros((2 * R, snaps.shape[1]), F32)
    for c in range(cols):
        load(c).wait()
        both = jnp.concatenate(split2(modes_t[:, c * count : (c + 1) * count]), axis=0)
        sh, sl = split2(snaps[c * count : (c + 1) * count, :])
        total += dot(both, sl) + dot(both, sh)
    mine = total[R:] + total[:R]
    share = R // GROUP
    for s in range(GROUP):
        cross[0, s] = mine[share * s : share * (s + 1), :]
    for k in order:
        cross_copy(k).start()
    for c in range(EARLY_CHUNKS, len(CHUNKS)):
        for k in order:
            block_copy(k, c).start()
    ridge_load.wait()
    scale = column_scale(ridge_ref, times)
    for k in order:
        cross_copy(k).wait_recv()
    for k in range(1, GROUP):
        near_copy(k).start()
    near[spot] = cross[:, spot]
    for k in range(1, GROUP):
        near_copy(k).wait_recv()
    far[plane] = jnp.sum(near[...], axis=0)
    for k in range(1, planes):
        far_copy(k).start()
    for k in range(1, planes):
        far_copy(k).wait_recv()
    whole[spot] = jnp.sum(far[...], axis=0) * (1.0 / nodes_total)
    for k in range(1, GROUP):
        whole_copy(k).start()
    for k in range(1, GROUP):
        whole_copy(k).wait_recv()
    width = snaps.shape[1]
    for c in range(cols):
        for s in range(GROUP):
            coords_ref[share * s : share * (s + 1), c * width : (c + 1) * width] = whole[s, c]

    coords = coords_ref[...]
    packed[...] = pack6(split3(coords))
    fill_feats(coords, scale, feats)
    rho = first_guess(feats, hmat, xmat)
    rho = lax.fori_loop(0, COARSE_STEPS, lambda _, r: coarse_step(hmat, xmat, r), rho)
    size = lax.fori_loop(0, FINE_STEPS, lambda _, r: fine_step(hmat, xmat), rho)
    size_ref[...] = jnp.broadcast_to(size, size_ref.shape)
    store_weights(feats, xmat, scale, wh_ref, wl_ref)

    for t in range(len(CHUNKS)):
        start, size = CHUNKS[t]
        for k in order:
            block_copy(k, t).wait_recv()
        if start < DONE[0] or start >= DONE[1]:
            continue
        base = pl.multiple_of(col * count + start, TILE)
        values = [snaps[pl.ds(base, size), :]]
        values += [blocks_ref[k, start : start + size, :] for k in range(cols - 1)]
        done_ref[:, start - DONE[0] : start - DONE[0] + size] = corrected(
            jnp.concatenate(values, axis=1), modes_t[:, pl.ds(base, size)], packed[...],
            wh_ref[...], wl_ref[...],
        )
    for k in range(1, cols):
        cross_copy(k).wait_send()
        for c in range(len(CHUNKS)):
            block_copy(k, c).wait_send()
    for k in range(1, GROUP):
        near_copy(k).wait_send()
        whole_copy(k).wait_send()
    for k in range(1, planes):
        far_copy(k).wait_send()


def exchange_and_weigh(snapshots, modes_t, ridge, nodes_total):
    cols = lax.axis_size("tm")
    planes = lax.axis_size("row") // GROUP
    nodes, width = snapshots.shape
    count, times = nodes // cols, cols * width
    piece = (cols, R // GROUP, width)
    dma = pltpu.SemaphoreType.DMA
    vmem = pl.BlockSpec(memory_space=pltpu.VMEM)
    far_away = pl.BlockSpec(memory_space=pltpu.HBM)
    shape = jax.ShapeDtypeStruct
    return pl.pallas_call(
        functools.partial(main_kernel, nodes_total),
        out_shape=[
            shape((cols - 1, count, width), F32),
            shape((R, times), F32),
            shape((FEAT, times), BF16),
            shape((FEAT, times), BF16),
            shape((8, 128), F32),
            shape((FEAT, DONE[1] - DONE[0]), F32),
        ],
        in_specs=[far_away] * 3,
        out_specs=[vmem] * 6,
        scratch_shapes=[
            pltpu.VMEM((nodes, width), F32),
            pltpu.VMEM((R, nodes), F32),
            pltpu.VMEM((cols, GROUP, R // GROUP, width), F32),
            pltpu.VMEM((GROUP,) + piece, F32),
            pltpu.VMEM((planes,) + piece, F32),
            pltpu.VMEM((GROUP,) + piece, F32),
            pltpu.VMEM((FEAT, times), F32),
            pltpu.VMEM((times, times), F32),
            pltpu.VMEM((times, times), F32),
            pltpu.VMEM((6 * R, times), BF16),
            dma((cols + 1,)),
            dma((cols,)), dma((cols,)),
            dma((GROUP,)), dma((GROUP,)),
            dma((planes,)), dma((planes,)),
            dma((GROUP,)), dma((GROUP,)),
            dma((cols, len(CHUNKS))), dma((cols, len(CHUNKS))),
            pltpu.VMEM((FEAT,), F32), dma,
        ],
        compiler_params=pltpu.CompilerParams(
            collective_id=0, has_side_effects=True, vmem_limit_bytes=44 * 2**20
        ),
        cost_estimate=pl.CostEstimate(flops=10**10, bytes_accessed=2**24, transcendentals=0),
    )(snapshots, modes_t, ridge)


def final_kernel(
    snaps_ref, modes_ref, ridge_ref, blocks_ref, coords_ref, wh_ref, wl_ref, size_ref, done_ref,
    *refs,
):
    early, refs = refs[:-12], refs[-12:]
    (
        out_ref, own, modes_t, result, wh_slow, wl_slow, feats, hmat, xmat,
        load_sem, done_sem, result_sem,
    ) = refs
    times = hmat.shape[0]
    parts, count, _ = blocks_ref.shape
    tiles = count // TILE
    first = lax.axis_index("tm") * count
    rest = [t for t in range(tiles) if not DONE[0] <= t * TILE < DONE[1]]

    def moves(slot, tile):
        rows = pl.ds(pl.multiple_of(first + tile * TILE, TILE), TILE)
        return (
            pltpu.make_async_copy(snaps_ref.at[rows, :], own.at[slot], load_sem.at[slot, 0]),
            pltpu.make_async_copy(modes_ref.at[:, rows], modes_t.at[slot], load_sem.at[slot, 1]),
        )

    def store(slot, tile):
        columns = pl.ds(pl.multiple_of(tile * TILE, TILE), TILE)
        return pltpu.make_async_copy(
            result.at[slot], out_ref.at[:, columns], result_sem.at[slot]
        )

    def compute(slot, tile, wh, wl):
        rows = pl.ds(pl.multiple_of(tile * TILE, TILE), TILE)
        if early and isinstance(tile, int) and tile == 0:
            others = [block[...] for block in early]
        else:
            others = [blocks_ref[k, rows, :] for k in range(parts)]
        result[slot] = corrected(
            jnp.concatenate([own[slot]] + others, axis=1), modes_t[slot],
            pack6(split3(coords_ref[...])), wh[...], wl[...],
        )

    copy = pltpu.make_async_copy(
        done_ref, out_ref.at[:, pl.ds(DONE[0], DONE[1] - DONE[0])], done_sem
    )
    for slot, tile in enumerate(rest):
        for move in moves(slot, tile):
            move.start()
    copy.start()
    good = jnp.max(size_ref[...]) <= FINE_STOP
    for slot, tile in enumerate(rest):
        for move in moves(slot, tile):
            move.wait()
        compute(slot, tile, wh_ref, wl_ref)
        store(slot, tile).start()
    for slot, tile in enumerate(rest):
        store(slot, tile).wait()
    copy.wait()

    @pl.when(jnp.logical_not(good))
    def _():
        scale = column_scale(ridge_ref, times)
        fill_feats(coords_ref[...], scale, feats)
        rho = jnp.max(first_guess(feats, hmat, xmat))
        lax.while_loop(lambda r: r > HIGH_STOP, lambda r: high_step(hmat, xmat, r), rho)
        lax.while_loop(
            lambda s: jnp.logical_and(s[0] < FINE_MAX, s[1] > FINE_STOP),
            lambda s: (s[0] + 1, jnp.max(fine_step(hmat, xmat))),
            (jnp.int32(0), jnp.float32(1.0)),
        )
        store_weights(feats, xmat, scale, wh_slow, wl_slow)

        def whole_tile(tile):
            for move in moves(0, tile):
                move.start()
            for move in moves(0, tile):
                move.wait()
            compute(0, tile, wh_slow, wl_slow)
            store(0, tile).start()
            store(0, tile).wait()

        whole_tile(0)
        lax.fori_loop(1, tiles, lambda tile, _: whole_tile(tile), None)


def finish(snapshots, modes_t, ridge, blocks, coords, wh, wl, size, done, early):
    parts, count, width = blocks.shape
    times = (parts + 1) * width
    slots = (count - DONE[1] + DONE[0]) // TILE
    dma = pltpu.SemaphoreType.DMA
    vmem = pl.BlockSpec(memory_space=pltpu.VMEM)
    far_away = pl.BlockSpec(memory_space=pltpu.HBM)
    return pl.pallas_call(
        final_kernel,
        out_shape=jax.ShapeDtypeStruct((FEAT, count), F32),
        in_specs=[far_away, far_away] + [vmem] * (7 + len(early)),
        out_specs=far_away,
        scratch_shapes=[
            pltpu.VMEM((slots, TILE, width), F32),
            pltpu.VMEM((slots, R, TILE), F32),
            pltpu.VMEM((slots, FEAT, TILE), F32),
            pltpu.VMEM((FEAT, times), BF16),
            pltpu.VMEM((FEAT, times), BF16),
            pltpu.VMEM((FEAT, times), F32),
            pltpu.VMEM((times, times), F32),
            pltpu.VMEM((times, times), F32),
            dma((slots, 2)), dma, dma((slots,)),
        ],
        compiler_params=pltpu.CompilerParams(vmem_limit_bytes=36 * 2**20),
        cost_estimate=pl.CostEstimate(flops=10**9, bytes_accessed=2**23, transcendentals=0),
    )(snapshots, modes_t, ridge, blocks, coords, wh, wl, size, done, *early)


def shards(snapshots, modes, ridge):
    nodes_total = modes.shape[0] * lax.axis_size("row")
    modes_t = modes.T
    early = []
    found = exchange_and_weigh(snapshots, modes_t, ridge, nodes_total)
    return finish(snapshots, modes_t, ridge, *found, early).T


def solution(mesh):
    return jax.shard_map(
        shards,
        mesh=mesh,
        in_specs=(P("row", "tm"), P("row", None), P()),
        out_specs=P(("row", "tm"), None),
        check_vma=False,
    )
```

```python
import functools

import jax
import jax.numpy as jnp
import numpy as np
from jax import lax
from jax.experimental import pallas as pl
from jax.experimental.pallas import tpu as pltpu
from jax.sharding import PartitionSpec as P

R = 32
FEAT = R * (R + 1) // 2
F32 = jnp.float32
BF16 = jnp.bfloat16
COARSE_STEPS = 5
FINE_STEPS = 2
FINE_STOP = 4e-3
HIGH_STOP = 0.05
FINE_MAX = 12
GROUP = 8
TILE = 128
CHUNKS = ((0, 256), (256, 256), (512, 512), (1024, 512), (1536, 256), (1792, 128), (1920, 128))
EARLY_CHUNKS = 0
DONE = (0, 1920)
MESH = pl.DeviceIdType.MESH


def split2(x):
    hi = x.astype(BF16)
    return hi, (x - hi.astype(F32)).astype(BF16)


def split3(x):
    hi = x.astype(BF16)
    rest = x - hi.astype(F32)
    mid = rest.astype(BF16)
    return hi, mid, (rest - mid.astype(F32)).astype(BF16)


def dot(a, b, dims=((1,), (0,))):
    return lax.dot_general(a, b, (dims, ((), ())), preferred_element_type=F32)


def dot3(a, b, dims=((1,), (0,))):
    ah, al = a
    bh, bl = b
    return dot(al, bh, dims) + dot(ah, bl, dims) + dot(ah, bh, dims)


def dot6(a, b, dims=((1,), (0,))):
    ah, am, al = a
    bh, bm, bl = b
    small = dot(al, bh, dims) + dot(ah, bl, dims) + dot(am, bm, dims)
    return small + (dot(am, bh, dims) + dot(ah, bm, dims)) + dot(ah, bh, dims)


def identity(size):
    down = lax.broadcasted_iota(jnp.int32, (size, size), 0)
    return (down == lax.broadcasted_iota(jnp.int32, (size, size), 1)).astype(F32)


def column_scale(ridge_ref, times):
    row = lax.rsqrt(ridge_ref[...].reshape(1, FEAT) * times)
    return jnp.sum(identity(FEAT) * row, axis=1, keepdims=True)


def pack6(parts):
    hi, mid, low = parts
    return jnp.concatenate([hi, mid, low, hi, mid, hi], axis=0)


def fill_feats(coords, scale, feats):
    start = 0
    for i in range(R):
        feats[start : start + R - i, :] = (
            coords[i : i + 1, :] * coords[i:, :] * scale[start : start + R - i, :]
        )
        start += R - i


def first_guess(feats, hmat, xmat):
    eye = identity(hmat.shape[0])
    scaled = feats[...]
    hmat[...] = eye + dot6(split3(scaled.T), split3(scaled))
    upper = jnp.max(jnp.sum(jnp.abs(hmat[...]), axis=0, keepdims=True), axis=1, keepdims=True)
    first = 2.0 / (1.0 + upper)
    rho = (upper - 1.0) * first * 0.5
    gain = 2.0 / (2.0 - rho * rho)
    xmat[...] = (gain * first) * (2.0 * eye - first * hmat[...])
    return rho * rho * 0.5 * gain


def coarse_step(hmat, xmat, rho):
    gain = 2.0 / (2.0 - rho * rho)
    x = xmat[...].astype(BF16)
    turn = 2.0 * identity(hmat.shape[0]) - dot(hmat[...].astype(BF16), x)
    xmat[...] = gain * dot(x, turn.astype(BF16))
    return rho * rho * 0.5 * gain


def high_step(hmat, xmat, rho):
    gain = 2.0 / (2.0 - rho * rho)
    x = split3(xmat[...])
    turn = 2.0 * identity(hmat.shape[0]) - dot6(split3(hmat[...]), x)
    xmat[...] = gain * dot6(x, split3(turn))
    return rho * rho * 0.5 * gain


def fine_step(hmat, xmat):
    x = xmat[...]
    rest = identity(hmat.shape[0]) - dot6(split3(hmat[...]), split3(x))
    xmat[...] = x + dot3(split2(x), split2(rest))
    return jnp.max(jnp.sum(jnp.abs(rest), axis=0, keepdims=True), axis=1, keepdims=True)


def store_weights(feats, xmat, scale, wh_ref, wl_ref):
    wh, wl = split2(dot6(split3(feats[...]), split3(xmat[...])) * scale)
    wh_ref[...] = wh
    wl_ref[...] = wl


def corrected(snaps, modes_t, packed, wh, wl):
    mh, mm, ml = split3(modes_t)
    modes6 = jnp.concatenate([mh, mh, mh, mm, mm, ml], axis=0)
    resid = snaps - dot(modes6, packed, ((0,), (0,)))
    rh, rl = split2(resid)
    last = ((1,), (1,))
    return dot(wh, rl, last) + dot(wl, rh, last) + dot(wh, rh, last)


def main_kernel(nodes_total, snaps_ref, modes_ref, ridge_hbm, *refs):
    (
        blocks_ref, coords_ref, wh_ref, wl_ref, size_ref, done_ref,
        snaps, modes_t, cross, near, far, whole, feats, hmat, xmat, packed,
        load_sem, cross_send, cross_recv, near_send, near_recv, far_send, far_recv,
        whole_send, whole_recv, block_send, block_recv, ridge_ref, ridge_sem,
    ) = refs
    row, col = lax.axis_index("row"), lax.axis_index("tm")
    cols, planes = cross.shape[0], far.shape[0]
    plane, spot = row // GROUP, row % GROUP
    count = snaps.shape[0] // cols
    times = hmat.shape[0]

    def cross_peer(k):
        return {"tm": (col + k) % cols}

    def near_peer(k):
        return {"row": plane * GROUP + (spot + k) % GROUP}

    def far_peer(k):
        return {"row": ((plane + k) % planes) * GROUP + spot}

    def remote(src, dst, send, recv, peer):
        return pltpu.make_async_remote_copy(
            src_ref=src, dst_ref=dst, send_sem=send, recv_sem=recv,
            device_id=peer, device_id_type=MESH,
        )

    def block_copy(k, c):
        start, size = CHUNKS[c]
        source = snaps_ref.at[pl.ds(((col + k) % cols) * count + start, size), :]
        return remote(
            source, blocks_ref.at[k - 1, pl.ds(start, size), :],
            block_send.at[k, c], block_recv.at[k, c], cross_peer(k),
        )

    def cross_copy(k):
        return remote(cross.at[0], cross.at[k], cross_send.at[k], cross_recv.at[k], cross_peer(k))

    def near_copy(k):
        return remote(
            cross.at[:, (spot + k) % GROUP], near.at[spot],
            near_send.at[k], near_recv.at[k], near_peer(k),
        )

    def far_copy(k):
        return remote(far.at[plane], far.at[plane], far_send.at[k], far_recv.at[k], far_peer(k))

    def whole_copy(k):
        return remote(
            whole.at[spot], whole.at[spot], whole_send.at[k], whole_recv.at[k], near_peer(k)
        )

    def load(c):
        rows = pl.ds(c * count, count)
        return pltpu.make_async_copy(snaps_ref.at[rows, :], snaps.at[rows, :], load_sem.at[c])

    barrier = pltpu.get_barrier_semaphore()
    peers = [far_peer(k) for k in range(1, planes)] + [cross_peer(k) for k in range(1, cols)]
    peers += [near_peer(k) for k in range(1, GROUP)]
    for peer in peers:
        pl.semaphore_signal(barrier, inc=1, device_id=peer, device_id_type=MESH)
    modes_load = pltpu.make_async_copy(modes_ref, modes_t, load_sem.at[cols])
    modes_load.start()
    ridge_load = pltpu.make_async_copy(ridge_hbm, ridge_ref, ridge_sem)
    ridge_load.start()
    for c in range(cols):
        load(c).start()

    order = [1, cols - 1] + list(range(2, cols - 1))
    modes_load.wait()
    total = jnp.zeros((2 * R, snaps.shape[1]), F32)
    for c in range(cols):
        load(c).wait()
        both = jnp.concatenate(split2(modes_t[:, c * count : (c + 1) * count]), axis=0)
        sh, sl = split2(snaps[c * count : (c + 1) * count, :])
        total += dot(both, sl) + dot(both, sh)
    mine = total[R:] + total[:R]
    share = R // GROUP
    for s in range(GROUP):
        cross[0, s] = mine[share * s : share * (s + 1), :]
    pl.semaphore_wait(barrier, len(peers))
    for k in order:
        cross_copy(k).start()
    for c in range(EARLY_CHUNKS, len(CHUNKS)):
        for k in order:
            block_copy(k, c).start()
    ridge_load.wait()
    scale = column_scale(ridge_ref, times)
    for k in order:
        cross_copy(k).wait_recv()
    for k in range(1, GROUP):
        near_copy(k).start()
    near[spot] = cross[:, spot]
    for k in range(1, GROUP):
        near_copy(k).wait_recv()
    far[plane] = jnp.sum(near[...], axis=0)
    for k in range(1, planes):
        far_copy(k).start()
    for k in range(1, planes):
        far_copy(k).wait_recv()
    whole[spot] = jnp.sum(far[...], axis=0) * (1.0 / nodes_total)
    for k in range(1, GROUP):
        whole_copy(k).start()
    for k in range(1, GROUP):
        whole_copy(k).wait_recv()
    width = snaps.shape[1]
    for c in range(cols):
        for s in range(GROUP):
            coords_ref[share * s : share * (s + 1), c * width : (c + 1) * width] = whole[s, c]

    coords = coords_ref[...]
    packed[...] = pack6(split3(coords))
    fill_feats(coords, scale, feats)
    rho = first_guess(feats, hmat, xmat)
    rho = lax.fori_loop(0, COARSE_STEPS, lambda _, r: coarse_step(hmat, xmat, r), rho)
    size = lax.fori_loop(0, FINE_STEPS, lambda _, r: fine_step(hmat, xmat), rho)
    size_ref[...] = jnp.broadcast_to(size, size_ref.shape)
    store_weights(feats, xmat, scale, wh_ref, wl_ref)

    for t in range(len(CHUNKS)):
        start, size = CHUNKS[t]
        for k in order:
            block_copy(k, t).wait_recv()
        if start < DONE[0] or start >= DONE[1]:
            continue
        base = pl.multiple_of(col * count + start, TILE)
        values = [snaps[pl.ds(base, size), :]]
        values += [blocks_ref[k, start : start + size, :] for k in range(cols - 1)]
        done_ref[:, start - DONE[0] : start - DONE[0] + size] = corrected(
            jnp.concatenate(values, axis=1), modes_t[:, pl.ds(base, size)], packed[...],
            wh_ref[...], wl_ref[...],
        )
    for k in range(1, cols):
        cross_copy(k).wait_send()
        for c in range(len(CHUNKS)):
            block_copy(k, c).wait_send()
    for k in range(1, GROUP):
        near_copy(k).wait_send()
        whole_copy(k).wait_send()
    for k in range(1, planes):
        far_copy(k).wait_send()


def exchange_and_weigh(snapshots, modes_t, ridge, nodes_total):
    cols = lax.axis_size("tm")
    planes = lax.axis_size("row") // GROUP
    nodes, width = snapshots.shape
    count, times = nodes // cols, cols * width
    piece = (cols, R // GROUP, width)
    dma = pltpu.SemaphoreType.DMA
    vmem = pl.BlockSpec(memory_space=pltpu.VMEM)
    far_away = pl.BlockSpec(memory_space=pltpu.HBM)
    shape = jax.ShapeDtypeStruct
    return pl.pallas_call(
        functools.partial(main_kernel, nodes_total),
        out_shape=[
            shape((cols - 1, count, width), F32),
            shape((R, times), F32),
            shape((FEAT, times), BF16),
            shape((FEAT, times), BF16),
            shape((8, 128), F32),
            shape((FEAT, DONE[1] - DONE[0]), F32),
        ],
        in_specs=[far_away] * 3,
        out_specs=[vmem] * 6,
        scratch_shapes=[
            pltpu.VMEM((nodes, width), F32),
            pltpu.VMEM((R, nodes), F32),
            pltpu.VMEM((cols, GROUP, R // GROUP, width), F32),
            pltpu.VMEM((GROUP,) + piece, F32),
            pltpu.VMEM((planes,) + piece, F32),
            pltpu.VMEM((GROUP,) + piece, F32),
            pltpu.VMEM((FEAT, times), F32),
            pltpu.VMEM((times, times), F32),
            pltpu.VMEM((times, times), F32),
            pltpu.VMEM((6 * R, times), BF16),
            dma((cols + 1,)),
            dma((cols,)), dma((cols,)),
            dma((GROUP,)), dma((GROUP,)),
            dma((planes,)), dma((planes,)),
            dma((GROUP,)), dma((GROUP,)),
            dma((cols, len(CHUNKS))), dma((cols, len(CHUNKS))),
            pltpu.VMEM((FEAT,), F32), dma,
        ],
        compiler_params=pltpu.CompilerParams(
            collective_id=0, has_side_effects=True, vmem_limit_bytes=44 * 2**20
        ),
        cost_estimate=pl.CostEstimate(flops=10**10, bytes_accessed=2**24, transcendentals=0),
    )(snapshots, modes_t, ridge)


def final_kernel(
    snaps_ref, modes_ref, ridge_ref, blocks_ref, coords_ref, wh_ref, wl_ref, size_ref, done_ref,
    *refs,
):
    early, refs = refs[:-12], refs[-12:]
    (
        out_ref, own, modes_t, result, wh_slow, wl_slow, feats, hmat, xmat,
        load_sem, done_sem, result_sem,
    ) = refs
    times = hmat.shape[0]
    parts, count, _ = blocks_ref.shape
    tiles = count // TILE
    first = lax.axis_index("tm") * count
    rest = [t for t in range(tiles) if not DONE[0] <= t * TILE < DONE[1]]

    def moves(slot, tile):
        rows = pl.ds(pl.multiple_of(first + tile * TILE, TILE), TILE)
        return (
            pltpu.make_async_copy(snaps_ref.at[rows, :], own.at[slot], load_sem.at[slot, 0]),
            pltpu.make_async_copy(modes_ref.at[:, rows], modes_t.at[slot], load_sem.at[slot, 1]),
        )

    def store(slot, tile):
        columns = pl.ds(pl.multiple_of(tile * TILE, TILE), TILE)
        return pltpu.make_async_copy(
            result.at[slot], out_ref.at[:, columns], result_sem.at[slot]
        )

    def compute(slot, tile, wh, wl):
        rows = pl.ds(pl.multiple_of(tile * TILE, TILE), TILE)
        if early and isinstance(tile, int) and tile == 0:
            others = [block[...] for block in early]
        else:
            others = [blocks_ref[k, rows, :] for k in range(parts)]
        result[slot] = corrected(
            jnp.concatenate([own[slot]] + others, axis=1), modes_t[slot],
            pack6(split3(coords_ref[...])), wh[...], wl[...],
        )

    copy = pltpu.make_async_copy(
        done_ref, out_ref.at[:, pl.ds(DONE[0], DONE[1] - DONE[0])], done_sem
    )
    for slot, tile in enumerate(rest):
        for move in moves(slot, tile):
            move.start()
    copy.start()
    good = jnp.max(size_ref[...]) <= FINE_STOP
    for slot, tile in enumerate(rest):
        for move in moves(slot, tile):
            move.wait()
        compute(slot, tile, wh_ref, wl_ref)
        store(slot, tile).start()
    for slot, tile in enumerate(rest):
        store(slot, tile).wait()
    copy.wait()

    @pl.when(jnp.logical_not(good))
    def _():
        scale = column_scale(ridge_ref, times)
        fill_feats(coords_ref[...], scale, feats)
        rho = jnp.max(first_guess(feats, hmat, xmat))
        lax.while_loop(lambda r: r > HIGH_STOP, lambda r: high_step(hmat, xmat, r), rho)
        lax.while_loop(
            lambda s: jnp.logical_and(s[0] < FINE_MAX, s[1] > FINE_STOP),
            lambda s: (s[0] + 1, jnp.max(fine_step(hmat, xmat))),
            (jnp.int32(0), jnp.float32(1.0)),
        )
        store_weights(feats, xmat, scale, wh_slow, wl_slow)

        def whole_tile(tile):
            for move in moves(0, tile):
                move.start()
            for move in moves(0, tile):
                move.wait()
            compute(0, tile, wh_slow, wl_slow)
            store(0, tile).start()
            store(0, tile).wait()

        whole_tile(0)
        lax.fori_loop(1, tiles, lambda tile, _: whole_tile(tile), None)


def finish(snapshots, modes_t, ridge, blocks, coords, wh, wl, size, done, early):
    parts, count, width = blocks.shape
    times = (parts + 1) * width
    slots = (count - DONE[1] + DONE[0]) // TILE
    dma = pltpu.SemaphoreType.DMA
    vmem = pl.BlockSpec(memory_space=pltpu.VMEM)
    far_away = pl.BlockSpec(memory_space=pltpu.HBM)
    return pl.pallas_call(
        final_kernel,
        out_shape=jax.ShapeDtypeStruct((FEAT, count), F32),
        in_specs=[far_away, far_away] + [vmem] * (7 + len(early)),
        out_specs=far_away,
        scratch_shapes=[
            pltpu.VMEM((slots, TILE, width), F32),
            pltpu.VMEM((slots, R, TILE), F32),
            pltpu.VMEM((slots, FEAT, TILE), F32),
            pltpu.VMEM((FEAT, times), BF16),
            pltpu.VMEM((FEAT, times), BF16),
            pltpu.VMEM((FEAT, times), F32),
            pltpu.VMEM((times, times), F32),
            pltpu.VMEM((times, times), F32),
            dma((slots, 2)), dma, dma((slots,)),
        ],
        compiler_params=pltpu.CompilerParams(vmem_limit_bytes=36 * 2**20),
        cost_estimate=pl.CostEstimate(flops=10**9, bytes_accessed=2**23, transcendentals=0),
    )(snapshots, modes_t, ridge, blocks, coords, wh, wl, size, done, *early)


def shards(snapshots, modes, ridge):
    nodes_total = modes.shape[0] * lax.axis_size("row")
    modes_t = modes.T
    early = []
    found = exchange_and_weigh(snapshots, modes_t, ridge, nodes_total)
    return finish(snapshots, modes_t, ridge, *found, early).T


def solution(mesh):
    return jax.shard_map(
        shards,
        mesh=mesh,
        in_specs=(P("row", "tm"), P("row", None), P()),
        out_specs=P(("row", "tm"), None),
        check_vma=False,
    )
```
